32 devices in a mesh: groups: 2 (over y), patch: 4 (over z), tensor: 4 (over x, core).
Axes of the slice: x: 2, y: 2, z: 4, core: 2. Of those that a mesh axis runs over, the one named last changes fastest.
Arguments:
- hidden: bfloat16 [1152, 3072], P(('groups', 'patch'), 'tensor'), parts along dimension 0, may hold values from -40 to 40
- modulation: bfloat16 [3, 3072], P(None, 'tensor'), may hold values from -3 to 3
- w_qkv: bfloat16 [3072, 8, 384], P('patch', 'tensor'), may hold values from -0.109375 to 0.109375
- w_out: bfloat16 [3072, 1024], P('patch', 'tensor'), may hold values from -0.1875 to 0.1875
- qk_gain: float32 [2, 8, 128], P(None, 'tensor'), may hold values from 0.5 to 100
- stale: bfloat16 [2, 1152, 1024], P(None, 'groups', 'tensor'), parts along dimension 1, may hold values from -6 to 6
- offsets: int32 [8], P(('groups', 'patch')), parts along dimension 0, may hold values from 0 to 384, as said below
- text_count: int32 [2], P('groups'), parts along dimension 0, may hold values from 1 to 64
- exponents: int32 [2, 8, 8], P(None, ('groups', 'patch'), 'tensor'), parts along dimension 1, may hold values from -9 to -4
Outputs:
- result: bfloat16 [1152, 3072], P(('groups', 'patch'), 'tensor'), parts along dimension 0
The draws below stay inside these ranges and needn't reach their ends.
There are 2 independent parts, one for each index of `groups`. The reference program is written for one: setup_inputs(seed, part) draws one part's arguments, and reference() takes and returns one part's arrays. A program takes and returns all parts, laid end to end along the dimension named above; an argument that names none is the same for every part. Nothing has to cross between parts.
Inputs may be any that keep to these rules, and one draw needn't show every extreme that they name: `offsets`: the image tokens of the patches start at distinct multiples of 128.
All inputs are finite; a program needn't handle non-finite values.
Results may differ from the reference program's by a relative error of at most 0.003.
The reference program's roundings to bfloat16 on the way (of `normed`, `query`, `change`, `rebuilt`, `weights` and `attended`) count: a program that leaves them out, or rounds other values in their place, can miss the bound.
Values may be sent and summed in bfloat16 or wider, within the bound.
A program may use at most 128 MiB of HBM per device.

```python
import math
import jax
import jax.numpy as jnp
from jax import lax

D = 3072
HEAD = 128
IMG_DEV = 128
TXT_DEV = 16
ROWS_DEV = 144
TOKENS = 576
TXT = 64
HEADS = 8
N_PATCH = 4


def draw_hidden(key, part):
    key = jax.random.fold_in(key, 11)
    key_vals, key_rows, key_cols = jax.random.split(key, 3)
    values = jax.random.truncated_normal(key_vals, -4.0, 4.0, (TOKENS, D), jnp.float32)
    row_scale = jnp.exp(jax.random.uniform(key_rows, (TOKENS, 1), jnp.float32, 0.0, math.log(10.0)))
    col_scale = jnp.exp(jax.random.uniform(key_cols, (1, D), jnp.float32, 0.0, math.log(10.0)))
    return (0.1 * values * row_scale * col_scale).astype(jnp.bfloat16)


def draw_qk_gain(key, part):
    key = jax.random.fold_in(key, 23)
    key_base = jax.random.fold_in(key, 0)
    base = jnp.exp(jax.random.uniform(key_base, (2, HEADS, HEAD), jnp.float32, math.log(0.5), math.log(2.0)))
    return base.astype(jnp.float32)


def draw_offsets(key, part):
    key = jax.random.fold_in(key, 37)
    order = jax.random.permutation(key, N_PATCH).astype(jnp.int32)
    return order * IMG_DEV


def touch_ends(drawn, own_key, least, largest):
    longest = drawn.shape.index(max(drawn.shape))
    spots = []
    for shift in (0, 1):
        where = [jax.random.randint(jax.random.fold_in(own_key, axis), (), 0, length) for axis, length in enumerate(drawn.shape)]
        where[longest] = (where[longest] + shift) % drawn.shape[longest]
        spots.append(tuple(where))
    return drawn.at[spots[0]].set(least).at[spots[1]].set(largest)


def level_of(rng, extent, pieces, smallest, high):
    loudness, own = 1.0, jax.random.fold_in(rng, 6)
    for position, blocks in pieces:
        draws = jnp.exp(jax.random.uniform(jax.random.fold_in(own, position), (blocks,), jnp.float32, smallest / len(pieces), high / len(pieces)))
        loudness = loudness * jnp.repeat(draws, extent[position] // blocks).reshape([-1 if axis == position else 1 for axis in range(len(extent))])
    return loudness


def scatter_about(key, shape, width, reach, cuts=(), kind=jnp.bfloat16):
    level = level_of(key, shape, cuts, -0.22, 0.18) if cuts else 1.0
    result = jax.random.normal(key, shape, jnp.float32) * width * level
    return jnp.minimum(jnp.maximum(result, -reach), reach).astype(kind)


def setup_inputs(seed: int = 0, part: int = 0) -> dict:
    key_list = jax.random.split(jax.random.key(seed), 10)
    own_keys = jax.random.split(jax.random.fold_in(key_list[9], part), 10)
    return {
        "hidden": draw_hidden(jax.random.fold_in(jax.random.fold_in(key_list[9], part), 71), part),
        "modulation": scatter_about(key_list[1], (3, D), 0.6, 3.0, ((1, 4),)),
        "w_qkv": scatter_about(key_list[2], (D, HEADS, 3 * HEAD), D ** -0.5, 0.109375, ((0, 4), (1, 4))),
        "w_out": scatter_about(key_list[3], (D, HEADS * HEAD), (HEADS * HEAD) ** -0.5, 0.1875, ((0, 4), (1, 4))),
        "qk_gain": draw_qk_gain(jax.random.fold_in(key_list[9], 71), part),
        "stale": scatter_about(own_keys[5], (2, TOKENS, HEADS * HEAD), 1.0, 6.0, ((2, 4),)),
        "offsets": draw_offsets(jax.random.fold_in(jax.random.fold_in(key_list[9], part), 71), part),
        "text_count": jax.random.randint(own_keys[7], (1,), 1, TXT + 1).astype(jnp.int32),
        "exponents": touch_ends(jax.random.randint(own_keys[8], (2, N_PATCH, HEADS), -9, -3), jax.random.fold_in(own_keys[8], 1), -9, (-3) - 1).astype(jnp.int32),
    }


def rotate(values, cosine, sine):
    half = values.shape[-1] // 2
    turned = jnp.concatenate([-values[..., half:], values[..., :half]], axis=-1)
    return values * cosine + turned * sine

def rms_scale(values, gain):
    return values * lax.rsqrt(lax.optimization_barrier(jnp.mean(values * values, axis=-1, keepdims=True)) + 1e-06) * gain

def reference(hidden, modulation, w_qkv, w_out, qk_gain, stale, offsets, text_count, exponents):
    xf = hidden.astype(jnp.float32)
    centred = xf - lax.optimization_barrier(jnp.mean(xf, axis=-1, keepdims=True))
    normed = centred * lax.rsqrt(lax.optimization_barrier(jnp.mean(centred * centred, axis=-1, keepdims=True)) + 1e-06)
    mods = modulation.astype(jnp.float32)
    normed = (normed * (1.0 + mods[1]) + mods[0]).astype(jnp.bfloat16)
    mixed = jnp.dot(normed, w_qkv.reshape(D, HEADS * 3 * HEAD), preferred_element_type=jnp.float32)
    mixed = mixed.reshape(TOKENS, HEADS, 3, HEAD)
    query = rms_scale(mixed[:, :, 0], qk_gain[0])
    key_new = rms_scale(mixed[:, :, 1], qk_gain[1])
    value_new = mixed[:, :, 2]
    index = jnp.arange(TOKENS, dtype=jnp.int32)
    within = index % ROWS_DEV
    patch_of = index // ROWS_DEV
    positions = jnp.where(within < TXT_DEV, 0, offsets[patch_of] + within - TXT_DEV).astype(jnp.float32)
    half = HEAD // 2
    freqs = jnp.power(10000.0, -jnp.arange(half, dtype=jnp.float32) / half)
    angle = positions[:, None] * freqs[None, :]
    cosine = jnp.concatenate([jnp.cos(angle), jnp.cos(angle)], axis=-1)[:, None, :]
    sine = jnp.concatenate([jnp.sin(angle), jnp.sin(angle)], axis=-1)[:, None, :]
    query = rotate(query, cosine, sine).astype(jnp.bfloat16)
    key_new = rotate(key_new, cosine, sine)
    fresh = jnp.stack([key_new, value_new]).reshape(2, TOKENS, HEADS * HEAD)
    limit = 127.0 * jnp.exp2(exponents.astype(jnp.float32))
    limit = jnp.repeat(jnp.repeat(limit, ROWS_DEV, axis=1), HEAD, axis=2)
    old = stale.astype(jnp.float32)
    change = jnp.clip(fresh - old, -limit, limit).astype(jnp.bfloat16)
    rebuilt = (old + change.astype(jnp.float32)).astype(jnp.bfloat16)
    usable = (within >= TXT_DEV) | (patch_of * TXT_DEV + within < text_count[0])
    keys = jnp.transpose(rebuilt[0].reshape(TOKENS, HEADS, HEAD), (1, 0, 2))
    values = jnp.transpose(rebuilt[1].reshape(TOKENS, HEADS, HEAD), (1, 0, 2))
    queries = jnp.transpose(query, (1, 0, 2))
    scale = HEAD ** (-0.5)

    def one_head(items):
        head_query, head_keys, head_values = items
        scores = lax.dot_general(head_query, head_keys, (((1,), (1,)), ((), ())), preferred_element_type=jnp.float32) * scale
        scores = jnp.where(usable[None, :], scores, -1e+30)
        peak = lax.optimization_barrier(jnp.max(scores, axis=-1, keepdims=True))
        weights = jnp.exp(scores - peak)
        weights = (weights / lax.optimization_barrier(jnp.sum(weights, axis=-1, keepdims=True))).astype(jnp.bfloat16)
        return jnp.dot(weights, head_values, preferred_element_type=jnp.float32)
    attended = lax.map(one_head, (queries, keys, values))
    attended = jnp.transpose(attended, (1, 0, 2)).reshape(TOKENS, HEADS * HEAD).astype(jnp.bfloat16)
    projected = jnp.dot(attended, w_out.T, preferred_element_type=jnp.float32)
    return (xf + mods[2] * projected).astype(jnp.bfloat16)
```

```python
import functools

import numpy as np
import jax
import jax.numpy as jnp
from jax import lax
from jax.experimental import pallas as pl
from jax.experimental.pallas import tpu as pltpu
from jax.sharding import PartitionSpec as P

TXT_DEV = 16
F32 = jnp.float32
BF16 = jnp.bfloat16
MESH = pl.DeviceIdType.MESH


def rotate(values, cosine, sine):
    half = values.shape[-1] // 2
    turned = jnp.concatenate([-values[..., half:], values[..., :half]], axis=-1)
    return values * cosine + turned * sine


def rms_scale(values, gain):
    return values * lax.rsqrt(jnp.mean(values * values, axis=-1, keepdims=True) + 1e-06) * gain


def plain_body(hidden, modulation, w_qkv, w_out, qk_gain, stale, offsets, text_count, exponents):
    rows = hidden.shape[0]
    own_width = hidden.shape[1]
    heads = w_qkv.shape[1]
    head = w_qkv.shape[2] // 3
    whole, mods = (
        lax.all_gather(hidden, "tensor", axis=1, tiled=True),
        lax.all_gather(modulation, "tensor", axis=1, tiled=True),
    )
    xf = whole.astype(jnp.float32)
    centred = xf - jnp.mean(xf, axis=-1, keepdims=True)
    normed = centred * lax.rsqrt(jnp.mean(centred * centred, axis=-1, keepdims=True) + 1e-06)
    mods = mods.astype(jnp.float32)
    normed = (normed * (1.0 + mods[1]) + mods[0]).astype(jnp.bfloat16)
    qkv_flat = w_qkv.reshape(w_qkv.shape[0], heads * 3 * head)
    mixed = jnp.dot(
        normed,
        lax.all_gather(qkv_flat, "patch", axis=0, tiled=True),
        preferred_element_type=jnp.float32,
    )
    mixed = mixed.reshape(rows, heads, 3, head)
    query = rms_scale(mixed[:, :, 0], qk_gain[0])
    key_new = rms_scale(mixed[:, :, 1], qk_gain[1])
    value_new = mixed[:, :, 2]
    local = jnp.arange(rows, dtype=jnp.int32)
    positions = jnp.where(local < TXT_DEV, 0, offsets[0] + local - TXT_DEV).astype(jnp.float32)
    half = head // 2
    freqs = jnp.power(10000.0, -jnp.arange(half, dtype=jnp.float32) / half)
    angle = positions[:, None] * freqs[None, :]
    cosine = jnp.concatenate([jnp.cos(angle), jnp.cos(angle)], axis=-1)[:, None, :]
    sine = jnp.concatenate([jnp.sin(angle), jnp.sin(angle)], axis=-1)[:, None, :]
    query = rotate(query, cosine, sine).astype(jnp.bfloat16)
    key_new = rotate(key_new, cosine, sine)
    fresh = jnp.stack([key_new, value_new]).reshape(2, rows, heads * head)
    mine = lax.dynamic_slice_in_dim(stale, lax.axis_index("patch") * rows, rows, 1).astype(
        jnp.float32
    )
    limit = 127.0 * jnp.exp2(exponents[:, 0, :].astype(jnp.float32))
    limit = jnp.repeat(limit, head, axis=1)[:, None, :]
    change = jnp.clip(fresh - mine, -limit, limit).astype(jnp.bfloat16)
    changes = lax.all_gather(change, "patch", axis=1, tiled=True)
    total = stale.shape[1]
    keys = (stale[0].astype(jnp.float32) + changes[0].astype(jnp.float32)).astype(jnp.bfloat16)
    values = (stale[1].astype(jnp.float32) + changes[1].astype(jnp.float32)).astype(jnp.bfloat16)
    keys = keys.reshape(total, heads, head)
    values = values.reshape(total, heads, head)
    index = jnp.arange(total, dtype=jnp.int32)
    within = index % rows
    usable = (within >= TXT_DEV) | (index // rows * TXT_DEV + within < text_count[0])
    scale = head ** (-0.5)
    pieces = []
    for slot in range(heads):
        scores = (
            lax.dot_general(
                query[:, slot],
                keys[:, slot],
                (((1,), (1,)), ((), ())),
                preferred_element_type=jnp.float32,
            )
            * scale
        )
        scores = jnp.where(usable[None, :], scores, -1e30)
        peak = jnp.max(scores, axis=-1, keepdims=True)
        weights = jnp.exp(scores - peak)
        weights = (weights / jnp.sum(weights, axis=-1, keepdims=True)).astype(jnp.bfloat16)
        pieces.append(jnp.dot(weights, values[:, slot], preferred_element_type=jnp.float32))
    attended = jnp.concatenate(pieces, axis=-1).astype(jnp.bfloat16)
    projected = lax.dot_general(
        attended,
        lax.all_gather(w_out, "patch", axis=0, tiled=True),
        (((1,), (1,)), ((), ())),
        preferred_element_type=jnp.float32,
    )
    summed = lax.psum(projected.astype(jnp.bfloat16), "tensor").astype(jnp.float32)
    share = lax.dynamic_slice_in_dim(summed, lax.axis_index("tensor") * own_width, own_width, 1)
    gate = modulation[2].astype(jnp.float32)
    return (hidden.astype(jnp.float32) + gate * share).astype(jnp.bfloat16)


def kernel(
    hidden, mods, w_qkv, w_out, gain, stale, freqs, offsets, text_count, exponents, out,
    hbuf, modbuf, wbuf, wobuf, metasrc, meta, stbuf, normed, mixed, cosbuf, sinbuf, kv, att, abuf, res, landed,
    h_send, h_recv, hf_send, m_send, m_recv, w_send, w_recv, wf_send, wo_send, wo_recv,
    me_send, me_recv, st_send, st_recv, kv_send, kv_recv, a_send, a_recv, r_send, r_recv,
):
    g = lax.axis_index("groups")
    z = lax.axis_index("patch")
    t = lax.axis_index("tensor")
    x = t // 2
    c = t % 2
    lead = z // 2
    rows, width = hidden.shape
    half_k = width // 2
    head = stale.shape[2] // 2
    mine = 2 * rows
    leading = c == lead

    def remote(src, dst, send, recv, device):
        return pltpu.make_async_remote_copy(
            src_ref=src, dst_ref=dst, send_sem=send, recv_sem=recv, device_id=device, device_id_type=MESH
        )

    sibling = (g, z, 2 * x + 1 - c)

    def arrived(ref, sem):
        remote(ref, ref, st_send.at[0], sem, sibling).wait_recv()

    def left(ref, sem):
        remote(ref, ref, sem, st_recv.at[0], sibling).wait_send()

    modbuf[t, 0:3, :] = mods[...].astype(F32)
    for hl in range(2):
        for kind in range(2):
            scale = jnp.exp2(jnp.full((1, head), exponents[kind, 0, hl], jnp.int32).astype(F32))
            scale = jnp.floor(scale * 65536.0 + 0.5) * (1.0 / 65536.0)
            metasrc[hl, kind : kind + 1, :] = 127.0 * scale
            metasrc[hl, 2 + kind : 3 + kind, :] = gain[kind, hl : hl + 1, :]
        metasrc[hl, 4:5, :] = jnp.full((1, head), offsets[0], jnp.int32).astype(F32)

    barrier = pltpu.get_barrier_semaphore()
    for dz in range(4):
        for dt in range(4):
            if dz or dt:
                pl.semaphore_signal(
                    barrier, inc=1, device_id=(g, (z + dz) % 4, (t + dt) % 4), device_id_type=MESH
                )
    for core in range(2):
        pl.semaphore_signal(barrier, inc=1, device_id=(1 - g, z, 2 * x + core), device_id_type=MESH)
    pl.semaphore_wait(barrier, 17)

    target = z // 2
    j_mine = z % 2

    for hl in range(2):
        zt = 2 * c + hl

        @pl.when(zt != z)
        def _():
            remote(
                w_qkv.at[pl.ds(g * half_k, half_k), pl.ds(hl * 3 * head, 3 * head)],
                wbuf.at[z, g],
                w_send.at[hl],
                w_recv.at[z, g],
                (g, zt, t),
            ).start()
            remote(metasrc.at[hl], meta.at[j_mine], me_send.at[hl], me_recv.at[j_mine],
                   (g, zt, 2 * x + target)).start()

    for d in range(1, 4):
        remote(hidden, hbuf.at[j_mine, t], h_send.at[d], h_recv.at[j_mine, t],
               (g, (z + d) % 4, 2 * x + target)).start()

    @pl.when(c != target)
    def _():
        remote(hidden, hbuf.at[j_mine, t], h_send.at[0], h_recv.at[j_mine, t], sibling).start()

    @pl.when(c == target)
    def _():
        hbuf[j_mine, t] = hidden[...]

    for d in range(1, 4):
        remote(modbuf.at[t], modbuf.at[t], m_send.at[d], m_recv.at[t], (g, z, (t + d) % 4)).start()

    for hl in range(2):
        @pl.when(jnp.logical_and(leading, z % 2 == hl))
        def _():
            for part in range(2):
                remote(
                    w_qkv.at[pl.ds(part * half_k, half_k), pl.ds(hl * 3 * head, 3 * head)],
                    wbuf.at[z, part],
                    w_send.at[2 + part],
                    w_recv.at[z, part],
                    sibling,
                ).start()
                wbuf[z, part] = w_qkv[pl.ds(part * half_k, half_k), pl.ds(hl * 3 * head, 3 * head)]
            remote(
                stale.at[:, pl.ds(pl.multiple_of((1 - c) * mine, 16), mine), pl.ds(hl * head, head)],
                stbuf, st_send.at[0], st_recv.at[0], sibling,
            ).start()
            stbuf[...] = stale[:, pl.ds(pl.multiple_of(c * mine, 16), mine), pl.ds(hl * head, head)]
            meta[hl] = metasrc[hl]

    def line_slot(j, cs):
        p = 2 * c + j
        ts = 2 * x + cs

        @pl.when(jnp.logical_not(jnp.logical_and(p == z, c == cs)))
        def _():
            arrived(hbuf.at[j, ts], h_recv.at[j, ts])

        remote(hbuf.at[j, ts], hbuf.at[j, ts], hf_send.at[j, cs], h_recv.at[j, ts],
               (g, z, 2 * (1 - x) + c)).start()

    def weight_slot(d):
        zs = (z + d) % 4

        @pl.when(leading)
        def _():
            arrived(wbuf.at[zs, g], w_recv.at[zs, g])
            for k, device in enumerate((
                (1 - g, z, t), (1 - g, z, 2 * x + 1 - c), sibling,
            )):
                remote(wbuf.at[zs, g], wbuf.at[zs, g], wf_send.at[d, k], w_recv.at[zs, g], device).start()

    weight_slot(1)
    line_slot(0, 0)
    line_slot(0, 1)
    weight_slot(3)
    line_slot(1, 0)
    line_slot(1, 1)
    weight_slot(2)

    wobuf[t] = w_out[...]
    for d in range(1, 4):
        remote(w_out, wobuf.at[t], wo_send.at[d], wo_recv.at[t], (g, z, (t + d) % 4)).start()

    place = lax.broadcasted_iota(jnp.int32, (rows, head), 0)
    lane = lax.broadcasted_iota(jnp.int32, (rows, head), 1)
    for j in range(2):
        @pl.when(jnp.logical_not(jnp.logical_and(leading, z % 2 == j)))
        def _():
            arrived(meta.at[j], me_recv.at[j])

        positions = jnp.where(place < TXT_DEV, 0.0, meta[j, 4:5, :] + (place - TXT_DEV).astype(F32))
        angle = positions * freqs[...]
        cosbuf[pl.ds(j * rows, rows), :] = jnp.cos(angle)
        sine = jnp.sin(angle)
        sinbuf[pl.ds(j * rows, rows), :] = jnp.where(lane < head // 2, -sine, sine)

    for d in range(1, 4):
        arrived(modbuf.at[(t + d) % 4], m_recv.at[(t + d) % 4])
    features = 4 * width
    for j in range(2):
        for cs in range(2):
            arrived(hbuf.at[j, 2 * (1 - x) + cs], h_recv.at[j, 2 * (1 - x) + cs])

        @pl.loop(0, rows // 16)
        def _(i):
            at = pl.ds(pl.multiple_of(i * 16, 16), 16)
            xs = [hbuf[j, k, at, :].astype(F32) for k in range(4)]
            total = sum(jnp.sum(v, axis=-1, keepdims=True) for v in xs)
            mean = total * (1.0 / features)
            xs = [v - mean for v in xs]
            total = sum(jnp.sum(v * v, axis=-1, keepdims=True) for v in xs)
            inverse = lax.rsqrt(total * (1.0 / features) + 1e-06)
            to = pl.ds(pl.multiple_of(j * rows + i * 16, 16), 16)
            for k in range(4):
                value = xs[k] * inverse * (1.0 + modbuf[k, 1:2, :]) + modbuf[k, 0:1, :]
                normed[to, pl.ds(k * width, width)] = value.astype(BF16)

    for zs in range(4):
        for part in range(2):
            own = jnp.logical_and(leading, jnp.logical_or(zs == z, g == part))

            @pl.when(jnp.logical_not(own))
            def _():
                arrived(wbuf.at[zs, part], w_recv.at[zs, part])

            value = jnp.dot(
                normed[:, pl.ds(zs * width + part * half_k, half_k)], wbuf[zs, part],
                preferred_element_type=F32,
            )
            if zs or part:
                mixed[...] += value
            else:
                mixed[...] = value

    @pl.when(jnp.logical_not(leading))
    def _():
        arrived(stbuf, st_recv.at[0])

    def rms(values, row):
        root = lax.rsqrt(jnp.mean(values * values, axis=-1, keepdims=True) + 1e-06)
        return values * root * meta[0, row : row + 1, :]

    def turn(values):
        return values * cosbuf[...] + pltpu.roll(values, head // 2, 1) * sinbuf[...]

    second = lax.broadcasted_iota(jnp.int32, (mine, head), 0) >= rows
    ours = pl.ds(pl.multiple_of(c * mine, 16), mine)
    key_new = turn(rms(mixed[:, head : 2 * head], 3))
    for kind, fresh in enumerate((key_new, mixed[:, 2 * head : 3 * head])):
        limit = jnp.where(second, meta[1, kind : kind + 1, :], meta[0, kind : kind + 1, :])
        old = stbuf[kind].astype(F32)
        change = jnp.clip(fresh - old, -limit, limit).astype(BF16)
        kv[kind, ours, :] = (old + change.astype(F32)).astype(BF16)
    remote(kv.at[:, ours, :], kv.at[:, ours, :], kv_send.at[0], kv_recv.at[0], sibling).start()
    query = turn(rms(mixed[:, 0:head], 2)).astype(BF16)
    theirs = pl.ds(pl.multiple_of((1 - c) * mine, 16), mine)
    arrived(kv.at[:, theirs, :], kv_recv.at[0])

    keys = kv[0]
    values = kv[1]
    index = lax.broadcasted_iota(jnp.int32, (1, 2 * mine), 1)
    within = index % rows
    usable = (within >= TXT_DEV) | (index // rows * TXT_DEV + within < text_count[0])
    my_head = 4 * x + z
    for j in range(2):
        scores = lax.dot_general(
            query[j * rows : (j + 1) * rows], keys, (((1,), (1,)), ((), ())), preferred_element_type=F32
        ) * (head ** (-0.5))
        scores = jnp.where(usable, scores, -1e30)
        peak = jnp.max(scores, axis=-1, keepdims=True)
        weights = jnp.exp(scores - peak)
        weights = (weights / jnp.sum(weights, axis=-1, keepdims=True)).astype(BF16)
        att[j] = jnp.dot(weights, values, preferred_element_type=F32).astype(BF16)
        for d in range(1, 4):
            remote(att.at[j], abuf.at[my_head], a_send.at[j, d], a_recv.at[my_head],
                   (g, (z + d) % 4, 2 * j + c)).start()

        @pl.when(x == j)
        def _():
            abuf[my_head] = att[j]

        @pl.when(x != j)
        def _():
            remote(att.at[j], abuf.at[my_head], a_send.at[j, 0], a_recv.at[my_head], (g, z, 2 * j + c)).start()

    for d in range(1, 4):
        arrived(wobuf.at[(t + d) % 4], wo_recv.at[(t + d) % 4])
    for h in range(8):
        @pl.when(h != my_head)
        def _():
            arrived(abuf.at[h], a_recv.at[h])

    total = None
    for k in range(4):
        pair = jnp.concatenate([abuf[2 * k], abuf[2 * k + 1]], axis=-1)
        value = lax.dot_general(pair, wobuf[k], (((1,), (1,)), ((), ())), preferred_element_type=F32)
        total = value if total is None else total + value
    res[...] = (hbuf[x, z].astype(F32) + modbuf[z, 2:3, :] * total).astype(BF16)
    owner = 2 * c + x
    home = jnp.logical_and(owner == z, z == t)

    @pl.when(home)
    def _():
        landed[...] = res[...]

    @pl.when(jnp.logical_not(home))
    def _():
        remote(res, landed, r_send.at[0], r_recv.at[0], (g, owner, z)).start()

    from_self = jnp.logical_and(t == z, 2 * (z % 2) + z // 2 == t)

    @pl.when(jnp.logical_not(from_self))
    def _():
        arrived(landed, r_recv.at[0])

    out[...] = landed[...]

    for hl in range(2):
        @pl.when(2 * c + hl != z)
        def _():
            left(wbuf.at[z, g], w_send.at[hl])
            left(metasrc.at[hl], me_send.at[hl])
    for d in range(1, 4):
        left(hidden, h_send.at[d])
        left(modbuf.at[t], m_send.at[d])
        left(w_out, wo_send.at[d])
        for j in range(2):
            left(att.at[j], a_send.at[j, d])

    @pl.when(c != target)
    def _():
        left(hidden, h_send.at[0])

    @pl.when(leading)
    def _():
        for part in range(2):
            left(wbuf.at[z, part], w_send.at[2 + part])
        left(stbuf, st_send.at[0])
        for d in range(1, 4):
            for k in range(3):
                left(wbuf.at[(z + d) % 4, g], wf_send.at[d, k])

    for j in range(2):
        for cs in range(2):
            left(hbuf.at[j, 2 * x + cs], hf_send.at[j, cs])

        @pl.when(x != j)
        def _():
            left(att.at[j], a_send.at[j, 0])
    left(kv.at[:, ours, :], kv_send.at[0])

    @pl.when(jnp.logical_not(home))
    def _():
        left(res, r_send.at[0])


def body(hidden, modulation, w_qkv, w_out, qk_gain, stale, offsets, text_count, exponents):
    rows, width = hidden.shape
    head = w_qkv.shape[2] // 3
    half = head // 2
    freqs = np.power(10000.0, -np.arange(half) / half).astype(np.float32)
    freqs = jnp.asarray(np.concatenate([freqs, freqs])[None])
    dma = pltpu.SemaphoreType.DMA
    vmem = pl.BlockSpec(memory_space=pltpu.VMEM)
    smem = pl.BlockSpec(memory_space=pltpu.SMEM)
    return pl.pallas_call(
        kernel,
        out_shape=jax.ShapeDtypeStruct((rows, width), BF16),
        in_specs=[vmem] * 7 + [smem] * 3,
        out_specs=vmem,
        scratch_shapes=[
            pltpu.VMEM((2, 4, rows, width), BF16),
            pltpu.VMEM((4, 8, width), F32),
            pltpu.VMEM((4, 2, width // 2, 3 * head), BF16),
            pltpu.VMEM((4, width, 2 * head), BF16),
            pltpu.VMEM((2, 8, head), F32),
            pltpu.VMEM((2, 8, head), F32),
            pltpu.VMEM((2, 2 * rows, head), BF16),
            pltpu.VMEM((2 * rows, 4 * width), BF16),
            pltpu.VMEM((2 * rows, 3 * head), F32),
            pltpu.VMEM((2 * rows, head), F32),
            pltpu.VMEM((2 * rows, head), F32),
            pltpu.VMEM((2, 4 * rows, head), BF16),
            pltpu.VMEM((2, rows, head), BF16),
            pltpu.VMEM((8, rows, head), BF16),
            pltpu.VMEM((rows, width), BF16),
            pltpu.VMEM((rows, width), BF16),
            dma((4,)), dma((2, 4)), dma((2, 2)), dma((4,)), dma((4,)),
            dma((4,)), dma((4, 2)), dma((4, 3)), dma((4,)), dma((4,)),
            dma((2,)), dma((2,)), dma((1,)), dma((1,)), dma((1,)), dma((1,)),
            dma((2, 4)), dma((8,)), dma((1,)), dma((1,)),
        ],
        compiler_params=pltpu.CompilerParams(
            collective_id=0, has_side_effects=True, vmem_limit_bytes=40 * 2**20
        ),
    )(
        hidden, modulation, w_qkv.reshape(w_qkv.shape[0], -1), w_out, qk_gain, stale, freqs,
        offsets, text_count, exponents,
    )


def solution(mesh):
    in_specs = (
        P(("groups", "patch"), "tensor"),
        P(None, "tensor"),
        P("patch", "tensor", None),
        P("patch", "tensor"),
        P(None, "tensor", None),
        P(None, "groups", "tensor"),
        P(("groups", "patch")),
        P("groups"),
        P(None, ("groups", "patch"), "tensor"),
    )
    out_specs = P(("groups", "patch"), "tensor")
    small = (mesh.shape["groups"], mesh.shape["patch"], mesh.shape["tensor"]) == (2, 4, 4)
    return jax.shard_map(
        body if small else plain_body, mesh=mesh, in_specs=in_specs, out_specs=out_specs, check_vma=False
    )
```

```python
import functools

import numpy as np
import jax
import jax.numpy as jnp
from jax import lax
from jax.experimental import pallas as pl
from jax.experimental.pallas import tpu as pltpu
from jax.sharding import PartitionSpec as P

TXT_DEV = 16
F32 = jnp.float32
BF16 = jnp.bfloat16
MESH = pl.DeviceIdType.MESH
CHUNKS = 3


def rotate(values, cosine, sine):
    half = values.shape[-1] // 2
    turned = jnp.concatenate([-values[..., half:], values[..., :half]], axis=-1)
    return values * cosine + turned * sine


def rms_scale(values, gain):
    return values * lax.rsqrt(jnp.mean(values * values, axis=-1, keepdims=True) + 1e-06) * gain


def plain_body(hidden, modulation, w_qkv, w_out, qk_gain, stale, offsets, text_count, exponents):
    rows = hidden.shape[0]
    own_width = hidden.shape[1]
    heads = w_qkv.shape[1]
    head = w_qkv.shape[2] // 3
    whole, mods = (
        lax.all_gather(hidden, "tensor", axis=1, tiled=True),
        lax.all_gather(modulation, "tensor", axis=1, tiled=True),
    )
    xf = whole.astype(jnp.float32)
    centred = xf - jnp.mean(xf, axis=-1, keepdims=True)
    normed = centred * lax.rsqrt(jnp.mean(centred * centred, axis=-1, keepdims=True) + 1e-06)
    mods = mods.astype(jnp.float32)
    normed = (normed * (1.0 + mods[1]) + mods[0]).astype(jnp.bfloat16)
    qkv_flat = w_qkv.reshape(w_qkv.shape[0], heads * 3 * head)
    mixed = jnp.dot(
        normed,
        lax.all_gather(qkv_flat, "patch", axis=0, tiled=True),
        preferred_element_type=jnp.float32,
    )
    mixed = mixed.reshape(rows, heads, 3, head)
    query = rms_scale(mixed[:, :, 0], qk_gain[0])
    key_new = rms_scale(mixed[:, :, 1], qk_gain[1])
    value_new = mixed[:, :, 2]
    local = jnp.arange(rows, dtype=jnp.int32)
    positions = jnp.where(local < TXT_DEV, 0, offsets[0] + local - TXT_DEV).astype(jnp.float32)
    half = head // 2
    freqs = jnp.power(10000.0, -jnp.arange(half, dtype=jnp.float32) / half)
    angle = positions[:, None] * freqs[None, :]
    cosine = jnp.concatenate([jnp.cos(angle), jnp.cos(angle)], axis=-1)[:, None, :]
    sine = jnp.concatenate([jnp.sin(angle), jnp.sin(angle)], axis=-1)[:, None, :]
    query = rotate(query, cosine, sine).astype(jnp.bfloat16)
    key_new = rotate(key_new, cosine, sine)
    fresh = jnp.stack([key_new, value_new]).reshape(2, rows, heads * head)
    mine = lax.dynamic_slice_in_dim(stale, lax.axis_index("patch") * rows, rows, 1).astype(
        jnp.float32
    )
    limit = 127.0 * jnp.exp2(exponents[:, 0, :].astype(jnp.float32))
    limit = jnp.repeat(limit, head, axis=1)[:, None, :]
    change = jnp.clip(fresh - mine, -limit, limit).astype(jnp.bfloat16)
    changes = lax.all_gather(change, "patch", axis=1, tiled=True)
    total = stale.shape[1]
    keys = (stale[0].astype(jnp.float32) + changes[0].astype(jnp.float32)).astype(jnp.bfloat16)
    values = (stale[1].astype(jnp.float32) + changes[1].astype(jnp.float32)).astype(jnp.bfloat16)
    keys = keys.reshape(total, heads, head)
    values = values.reshape(total, heads, head)
    index = jnp.arange(total, dtype=jnp.int32)
    within = index % rows
    usable = (within >= TXT_DEV) | (index // rows * TXT_DEV + within < text_count[0])
    scale = head ** (-0.5)
    pieces = []
    for slot in range(heads):
        scores = (
            lax.dot_general(
                query[:, slot],
                keys[:, slot],
                (((1,), (1,)), ((), ())),
                preferred_element_type=jnp.float32,
            )
            * scale
        )
        scores = jnp.where(usable[None, :], scores, -1e30)
        peak = jnp.max(scores, axis=-1, keepdims=True)
        weights = jnp.exp(scores - peak)
        weights = (weights / jnp.sum(weights, axis=-1, keepdims=True)).astype(jnp.bfloat16)
        pieces.append(jnp.dot(weights, values[:, slot], preferred_element_type=jnp.float32))
    attended = jnp.concatenate(pieces, axis=-1).astype(jnp.bfloat16)
    projected = lax.dot_general(
        attended,
        lax.all_gather(w_out, "patch", axis=0, tiled=True),
        (((1,), (1,)), ((), ())),
        preferred_element_type=jnp.float32,
    )
    summed = lax.psum(projected.astype(jnp.bfloat16), "tensor").astype(jnp.float32)
    share = lax.dynamic_slice_in_dim(summed, lax.axis_index("tensor") * own_width, own_width, 1)
    gate = modulation[2].astype(jnp.float32)
    return (hidden.astype(jnp.float32) + gate * share).astype(jnp.bfloat16)


def kernel(
    hidden, mods, w_qkv, w_out, gain, stale, freqs, offsets, text_count, exponents, out,
    hbuf, modbuf, wbuf, wobuf, metasrc, meta, stbuf, normed, mixed, cosbuf, sinbuf, kv, att, abuf, res, landed,
    h_send, h_recv, hf_send, m_send, m_recv, w_send, w_recv, wl_send, wf_send, wo_send, wo_recv,
    me_send, me_recv, st_send, st_recv, kv_send, kv_recv, a_send, a_recv, r_send, r_recv,
):
    g = lax.axis_index("groups")
    z = lax.axis_index("patch")
    t = lax.axis_index("tensor")
    x = t // 2
    c = t % 2
    lead = z // 2
    rows, width = hidden.shape
    quarter = width // 4
    chunk = rows // CHUNKS
    head = stale.shape[2] // 2
    mine = 2 * rows
    leading = c == lead

    def remote(src, dst, send, recv, device):
        return pltpu.make_async_remote_copy(
            src_ref=src, dst_ref=dst, send_sem=send, recv_sem=recv, device_id=device, device_id_type=MESH
        )

    sibling = (g, z, 2 * x + 1 - c)

    def arrived(ref, sem):
        remote(ref, ref, st_send.at[0], sem, sibling).wait_recv()

    def left(ref, sem):
        remote(ref, ref, sem, st_recv.at[0], sibling).wait_send()

    modbuf[t, 0:3, :] = mods[...].astype(F32)
    for hl in range(2):
        for kind in range(2):
            scale = jnp.exp2(jnp.full((1, head), exponents[kind, 0, hl], jnp.int32).astype(F32))
            scale = jnp.floor(scale * 65536.0 + 0.5) * (1.0 / 65536.0)
            metasrc[hl, kind : kind + 1, :] = 127.0 * scale
            metasrc[hl, 2 + kind : 3 + kind, :] = gain[kind, hl : hl + 1, :]
        metasrc[hl, 4:5, :] = jnp.full((1, head), offsets[0], jnp.int32).astype(F32)

    barrier = pltpu.get_barrier_semaphore()
    for dz in range(4):
        for dt in range(4):
            if dz or dt:
                pl.semaphore_signal(
                    barrier, inc=1, device_id=(g, (z + dz) % 4, (t + dt) % 4), device_id_type=MESH
                )
    pl.semaphore_signal(barrier, inc=1, device_id=(1 - g, z, t), device_id_type=MESH)
    pl.semaphore_wait(barrier, 16)

    target = z // 2
    j_mine = z % 2

    def part_of(j, ts, k):
        return hbuf.at[j, ts, pl.ds(k * chunk, chunk)]

    for k in range(CHUNKS):
        piece = hidden.at[pl.ds(k * chunk, chunk)]
        place = part_of(j_mine, t, k)
        got = h_recv.at[j_mine, t, k]

        @pl.when(z < 3)
        def _():
            remote(piece, place, h_send.at[0, k], got, (g, z + 1, 2 * x + target)).start()

        @pl.when(z > 0)
        def _():
            remote(piece, place, h_send.at[1, k], got, (g, z - 1, 2 * x + target)).start()

        remote(piece, place, h_send.at[2, k], got, (g, z, 2 * (1 - x) + target)).start()

        @pl.when(c != target)
        def _():
            remote(piece, place, h_send.at[3, k], got, sibling).start()

    for hl in range(2):
        zt = 2 * c + hl

        @pl.when(zt != z)
        def _():
            for core in range(2):
                remote(
                    w_qkv.at[pl.ds((2 * g + core) * quarter, quarter), pl.ds(hl * 3 * head, 3 * head)],
                    wbuf.at[z, 2 * g + core],
                    w_send.at[hl, core],
                    w_recv.at[z, 2 * g + core],
                    (g, zt, 2 * x + core),
                ).start()
            remote(metasrc.at[hl], meta.at[j_mine], me_send.at[hl], me_recv.at[j_mine],
                   (g, zt, 2 * x + target)).start()

    for d in range(1, 4):
        remote(modbuf.at[t], modbuf.at[t], m_send.at[d], m_recv.at[t], (g, z, (t + d) % 4)).start()

    for hl in range(2):
        @pl.when(jnp.logical_and(leading, z % 2 == hl))
        def _():
            for part in range(4):
                remote(
                    w_qkv.at[pl.ds(part * quarter, quarter), pl.ds(hl * 3 * head, 3 * head)],
                    wbuf.at[z, part],
                    wl_send.at[part],
                    w_recv.at[z, part],
                    sibling,
                ).start()
                wbuf[z, part] = w_qkv[pl.ds(part * quarter, quarter), pl.ds(hl * 3 * head, 3 * head)]
            remote(
                stale.at[:, pl.ds(pl.multiple_of((1 - c) * mine, 16), mine), pl.ds(hl * head, head)],
                stbuf, st_send.at[0], st_recv.at[0], sibling,
            ).start()
            stbuf[...] = stale[:, pl.ds(pl.multiple_of(c * mine, 16), mine), pl.ds(hl * head, head)]
            meta[hl] = metasrc[hl]

    @pl.when(c == target)
    def _():
        hbuf[j_mine, t] = hidden[...]

    half_out = width // 2
    across = 2 * (1 - x) + c

    def send_out():
        remote(
            w_out.at[pl.ds(g * half_out, half_out)], wobuf.at[t, g], wo_send.at[0], wo_recv.at[t, g],
            (g, z, across),
        ).start()
        for part in range(2):
            remote(
                w_out.at[pl.ds(part * half_out, half_out)], wobuf.at[t, part], wo_send.at[1 + part],
                wo_recv.at[t, part], sibling,
            ).start()
            wobuf[t, part] = w_out[pl.ds(part * half_out, half_out)]

    def pass_out():
        slot, got = wobuf.at[across, g], wo_recv.at[across, g]
        arrived(slot, got)
        remote(slot, slot, wo_send.at[3], got, (1 - g, z, t)).start()
        remote(slot, slot, wo_send.at[4], got, sibling).start()

    def pass_out_far():
        slot, got = wobuf.at[across, 1 - g], wo_recv.at[across, 1 - g]
        arrived(slot, got)
        remote(slot, slot, wo_send.at[5], got, sibling).start()

    first_j = jnp.where(c == 0, jnp.where(z == 0, 0, 1), jnp.where(z == 3, 1, 0))

    def pass_hidden(order):
        j = first_j if order == 0 else 1 - first_j
        p = 2 * c + j
        onward = jnp.where(z > p, z + 1, z - 1)

        @pl.when(p != z)
        def _():
            for k in range(CHUNKS):
                for cs in range(2):
                    slot, got = part_of(j, 2 * x + cs, k), h_recv.at[j, 2 * x + cs, k]
                    arrived(slot, got)

                    @pl.when(jnp.logical_and(onward >= 0, onward < 4))
                    def _():
                        remote(slot, slot, hf_send.at[order, cs, k, 0], got, (g, (onward + 4) % 4, t)).start()

                    remote(slot, slot, hf_send.at[order, cs, k, 1], got, (g, z, across)).start()

    def pass_weight(d):
        zs = (z + d) % 4
        slot, got = wbuf.at[zs, 2 * g + c], w_recv.at[zs, 2 * g + c]
        arrived(slot, got)
        remote(slot, slot, wf_send.at[d, 0], got, (1 - g, z, t)).start()
        remote(slot, slot, wf_send.at[d, 1], got, sibling).start()

    def pass_weight_far(d):
        zs = (z + d) % 4
        slot, got = wbuf.at[zs, 2 * (1 - g) + c], w_recv.at[zs, 2 * (1 - g) + c]
        arrived(slot, got)
        remote(slot, slot, wf_send.at[d, 2], got, sibling).start()

    pass_hidden(0)
    pass_weight(1)
    pass_weight(3)
    pass_hidden(1)
    pass_weight(2)
    send_out()
    for d in (1, 3, 2):
        pass_weight_far(d)

    place = lax.broadcasted_iota(jnp.int32, (rows, head), 0)
    lane = lax.broadcasted_iota(jnp.int32, (rows, head), 1)
    for j in range(2):
        @pl.when(jnp.logical_not(jnp.logical_and(leading, z % 2 == j)))
        def _():
            arrived(meta.at[j], me_recv.at[j])

        positions = jnp.where(place < TXT_DEV, 0.0, meta[j, 4:5, :] + (place - TXT_DEV).astype(F32))
        angle = positions * freqs[...]
        cosbuf[pl.ds(j * rows, rows), :] = jnp.cos(angle)
        sine = jnp.sin(angle)
        sinbuf[pl.ds(j * rows, rows), :] = jnp.where(lane < head // 2, -sine, sine)

    for d in range(1, 4):
        arrived(modbuf.at[(t + d) % 4], m_recv.at[(t + d) % 4])
    features = 4 * width
    for j in range(2):
        for k in range(CHUNKS):
            for cs in range(2):
                arrived(part_of(j, 2 * (1 - x) + cs, k), h_recv.at[j, 2 * (1 - x) + cs, k])

            @pl.when(z == 2 * c + j)
            def _():
                arrived(part_of(j, 2 * x + 1 - c, k), h_recv.at[j, 2 * x + 1 - c, k])

        @pl.loop(0, rows // 16)
        def _(i):
            at = pl.ds(pl.multiple_of(i * 16, 16), 16)
            xs = [hbuf[j, k, at, :].astype(F32) for k in range(4)]
            total = sum(jnp.sum(v, axis=-1, keepdims=True) for v in xs)
            mean = total * (1.0 / features)
            xs = [v - mean for v in xs]
            total = sum(jnp.sum(v * v, axis=-1, keepdims=True) for v in xs)
            inverse = lax.rsqrt(total * (1.0 / features) + 1e-06)
            to = pl.ds(pl.multiple_of(j * rows + i * 16, 16), 16)
            for k in range(4):
                value = xs[k] * inverse * (1.0 + modbuf[k, 1:2, :]) + modbuf[k, 0:1, :]
                normed[to, pl.ds(k * width, width)] = value.astype(BF16)

    for zs in range(4):
        for core in range(2):
            quarter_at = 2 * core + 1 - c

            @pl.when(jnp.logical_not(jnp.logical_and(leading, zs == z)))
            def _():
                arrived(wbuf.at[zs, quarter_at], w_recv.at[zs, quarter_at])

            @pl.when(jnp.logical_and(jnp.logical_not(leading), zs == z))
            def _():
                arrived(wbuf.at[zs, 2 * core + c], w_recv.at[zs, 2 * core + c])

        value = jnp.dot(
            normed[:, pl.ds(zs * width, width)], wbuf[zs].reshape(width, 3 * head), preferred_element_type=F32
        )
        if zs:
            mixed[...] += value
        else:
            mixed[...] = value
    pass_out()

    @pl.when(jnp.logical_not(leading))
    def _():
        arrived(stbuf, st_recv.at[0])

    def rms(values, row):
        root = lax.rsqrt(jnp.mean(values * values, axis=-1, keepdims=True) + 1e-06)
        return values * root * meta[0, row : row + 1, :]

    def turn(values):
        return values * cosbuf[...] + pltpu.roll(values, head // 2, 1) * sinbuf[...]

    second = lax.broadcasted_iota(jnp.int32, (mine, head), 0) >= rows
    ours = pl.ds(pl.multiple_of(c * mine, 16), mine)
    key_new = turn(rms(mixed[:, head : 2 * head], 3))
    for kind, fresh in enumerate((key_new, mixed[:, 2 * head : 3 * head])):
        limit = jnp.where(second, meta[1, kind : kind + 1, :], meta[0, kind : kind + 1, :])
        old = stbuf[kind].astype(F32)
        change = jnp.clip(fresh - old, -limit, limit).astype(BF16)
        kv[kind, ours, :] = (old + change.astype(F32)).astype(BF16)
    remote(kv.at[:, ours, :], kv.at[:, ours, :], kv_send.at[0], kv_recv.at[0], sibling).start()
    query = turn(rms(mixed[:, 0:head], 2)).astype(BF16)
    pass_out_far()
    theirs = pl.ds(pl.multiple_of((1 - c) * mine, 16), mine)
    arrived(kv.at[:, theirs, :], kv_recv.at[0])

    keys = kv[0]
    values = kv[1]
    index = lax.broadcasted_iota(jnp.int32, (1, 2 * mine), 1)
    within = index % rows
    usable = (within >= TXT_DEV) | (index // rows * TXT_DEV + within < text_count[0])
    my_head = 4 * x + z
    for j in range(2):
        scores = lax.dot_general(
            query[j * rows : (j + 1) * rows], keys, (((1,), (1,)), ((), ())), preferred_element_type=F32
        ) * (head ** (-0.5))
        scores = jnp.where(usable, scores, -1e30)
        peak = jnp.max(scores, axis=-1, keepdims=True)
        weights = jnp.exp(scores - peak)
        weights = (weights / jnp.sum(weights, axis=-1, keepdims=True)).astype(BF16)
        att[j] = jnp.dot(weights, values, preferred_element_type=F32).astype(BF16)
        for d in range(1, 4):
            remote(att.at[j], abuf.at[my_head], a_send.at[j, d], a_recv.at[my_head],
                   (g, (z + d) % 4, 2 * j + c)).start()

        @pl.when(x == j)
        def _():
            abuf[my_head] = att[j]

        @pl.when(x != j)
        def _():
            remote(att.at[j], abuf.at[my_head], a_send.at[j, 0], a_recv.at[my_head], (g, z, 2 * j + c)).start()

    for part in range(2):
        for ts in (2 * x + 1 - c, 2 * (1 - x) + 1 - c):
            arrived(wobuf.at[ts, part], wo_recv.at[ts, part])
    for h in range(8):
        @pl.when(h != my_head)
        def _():
            arrived(abuf.at[h], a_recv.at[h])

    total = None
    for k in range(4):
        pair = jnp.concatenate([abuf[2 * k], abuf[2 * k + 1]], axis=-1)
        value = lax.dot_general(pair, wobuf[k].reshape(width, 2 * head), (((1,), (1,)), ((), ())), preferred_element_type=F32)
        total = value if total is None else total + value
    res[...] = (hbuf[x, z].astype(F32) + modbuf[z, 2:3, :] * total).astype(BF16)
    owner = 2 * c + x
    home = jnp.logical_and(owner == z, z == t)

    @pl.when(home)
    def _():
        landed[...] = res[...]

    @pl.when(jnp.logical_not(home))
    def _():
        remote(res, landed, r_send.at[0], r_recv.at[0], (g, owner, z)).start()

    from_self = jnp.logical_and(t == z, 2 * (z % 2) + z // 2 == t)

    @pl.when(jnp.logical_not(from_self))
    def _():
        arrived(landed, r_recv.at[0])

    out[...] = landed[...]

    for hl in range(2):
        @pl.when(2 * c + hl != z)
        def _():
            for core in range(2):
                left(wbuf.at[z, 2 * g + core], w_send.at[hl, core])
            left(metasrc.at[hl], me_send.at[hl])
    for d in range(1, 4):
        left(modbuf.at[t], m_send.at[d])
        for k in range(2):
            left(wbuf.at[(z + d) % 4, 2 * g + c], wf_send.at[d, k])
        left(wbuf.at[(z + d) % 4, 2 * (1 - g) + c], wf_send.at[d, 2])
        for j in range(2):
            left(att.at[j], a_send.at[j, d])
    for k in range(6):
        left(wobuf.at[t, 0], wo_send.at[k])
    for k in range(CHUNKS):
        piece = hidden.at[pl.ds(k * chunk, chunk)]

        @pl.when(z < 3)
        def _():
            left(piece, h_send.at[0, k])

        @pl.when(z > 0)
        def _():
            left(piece, h_send.at[1, k])

        left(piece, h_send.at[2, k])

        @pl.when(c != target)
        def _():
            left(piece, h_send.at[3, k])

    @pl.when(leading)
    def _():
        for part in range(4):
            left(wbuf.at[z, part], wl_send.at[part])
        left(stbuf, st_send.at[0])

    for order in range(2):
        j = first_j if order == 0 else 1 - first_j
        p = 2 * c + j
        onward = jnp.where(z > p, z + 1, z - 1)

        @pl.when(p != z)
        def _():
            for k in range(CHUNKS):
                for cs in range(2):
                    slot = part_of(j, 2 * x + cs, k)

                    @pl.when(jnp.logical_and(onward >= 0, onward < 4))
                    def _():
                        left(slot, hf_send.at[order, cs, k, 0])

                    left(slot, hf_send.at[order, cs, k, 1])

    for j in range(2):
        @pl.when(x != j)
        def _():
            left(att.at[j], a_send.at[j, 0])
    left(kv.at[:, ours, :], kv_send.at[0])

    @pl.when(jnp.logical_not(home))
    def _():
        left(res, r_send.at[0])


def body(hidden, modulation, w_qkv, w_out, qk_gain, stale, offsets, text_count, exponents):
    rows, width = hidden.shape
    head = w_qkv.shape[2] // 3
    half = head // 2
    freqs = np.power(10000.0, -np.arange(half) / half).astype(np.float32)
    freqs = jnp.asarray(np.concatenate([freqs, freqs])[None])
    dma = pltpu.SemaphoreType.DMA
    vmem = pl.BlockSpec(memory_space=pltpu.VMEM)
    smem = pl.BlockSpec(memory_space=pltpu.SMEM)
    return pl.pallas_call(
        kernel,
        out_shape=jax.ShapeDtypeStruct((rows, width), BF16),
        in_specs=[vmem] * 7 + [smem] * 3,
        out_specs=vmem,
        scratch_shapes=[
            pltpu.VMEM((2, 4, rows, width), BF16),
            pltpu.VMEM((4, 8, width), F32),
            pltpu.VMEM((4, 4, width // 4, 3 * head), BF16),
            pltpu.VMEM((4, 2, width // 2, 2 * head), BF16),
            pltpu.VMEM((2, 8, head), F32),
            pltpu.VMEM((2, 8, head), F32),
            pltpu.VMEM((2, 2 * rows, head), BF16),
            pltpu.VMEM((2 * rows, 4 * width), BF16),
            pltpu.VMEM((2 * rows, 3 * head), F32),
            pltpu.VMEM((2 * rows, head), F32),
            pltpu.VMEM((2 * rows, head), F32),
            pltpu.VMEM((2, 4 * rows, head), BF16),
            pltpu.VMEM((2, rows, head), BF16),
            pltpu.VMEM((8, rows, head), BF16),
            pltpu.VMEM((rows, width), BF16),
            pltpu.VMEM((rows, width), BF16),
            dma((4, CHUNKS)), dma((2, 4, CHUNKS)), dma((2, 2, CHUNKS, 2)), dma((4,)), dma((4,)),
            dma((2, 2)), dma((4, 4)), dma((4,)), dma((4, 3)), dma((6,)), dma((4, 2)),
            dma((2,)), dma((2,)), dma((1,)), dma((1,)), dma((1,)), dma((1,)),
            dma((2, 4)), dma((8,)), dma((1,)), dma((1,)),
        ],
        compiler_params=pltpu.CompilerParams(
            collective_id=0, has_side_effects=True, vmem_limit_bytes=40 * 2**20
        ),
    )(
        hidden, modulation, w_qkv.reshape(w_qkv.shape[0], -1), w_out, qk_gain, stale, freqs,
        offsets, text_count, exponents,
    )


def solution(mesh):
    in_specs = (
        P(("groups", "patch"), "tensor"),
        P(None, "tensor"),
        P("patch", "tensor", None),
        P("patch", "tensor"),
        P(None, "tensor", None),
        P(None, "groups", "tensor"),
        P(("groups", "patch")),
        P("groups"),
        P(None, ("groups", "patch"), "tensor"),
    )
    out_specs = P(("groups", "patch"), "tensor")
    small = (mesh.shape["groups"], mesh.shape["patch"], mesh.shape["tensor"]) == (2, 4, 4)
    return jax.shard_map(
        body if small else plain_body, mesh=mesh, in_specs=in_specs, out_specs=out_specs, check_vma=False
    )
```

```python
import functools

import numpy as np
import jax
import jax.numpy as jnp
from jax import lax
from jax.experimental import pallas as pl
from jax.experimental.pallas import tpu as pltpu
from jax.sharding import PartitionSpec as P

TXT_DEV = 16
F32 = jnp.float32
BF16 = jnp.bfloat16
MESH = pl.DeviceIdType.MESH
CHUNKS = 3
BANDS = 1


def rotate(values, cosine, sine):
    half = values.shape[-1] // 2
    turned = jnp.concatenate([-values[..., half:], values[..., :half]], axis=-1)
    return values * cosine + turned * sine


def rms_scale(values, gain):
    return values * lax.rsqrt(jnp.mean(values * values, axis=-1, keepdims=True) + 1e-06) * gain


def plain_body(hidden, modulation, w_qkv, w_out, qk_gain, stale, offsets, text_count, exponents):
    rows = hidden.shape[0]
    own_width = hidden.shape[1]
    heads = w_qkv.shape[1]
    head = w_qkv.shape[2] // 3
    whole, mods = (
        lax.all_gather(hidden, "tensor", axis=1, tiled=True),
        lax.all_gather(modulation, "tensor", axis=1, tiled=True),
    )
    xf = whole.astype(jnp.float32)
    centred = xf - jnp.mean(xf, axis=-1, keepdims=True)
    normed = centred * lax.rsqrt(jnp.mean(centred * centred, axis=-1, keepdims=True) + 1e-06)
    mods = mods.astype(jnp.float32)
    normed = (normed * (1.0 + mods[1]) + mods[0]).astype(jnp.bfloat16)
    qkv_flat = w_qkv.reshape(w_qkv.shape[0], heads * 3 * head)
    mixed = jnp.dot(
        normed,
        lax.all_gather(qkv_flat, "patch", axis=0, tiled=True),
        preferred_element_type=jnp.float32,
    )
    mixed = mixed.reshape(rows, heads, 3, head)
    query = rms_scale(mixed[:, :, 0], qk_gain[0])
    key_new = rms_scale(mixed[:, :, 1], qk_gain[1])
    value_new = mixed[:, :, 2]
    local = jnp.arange(rows, dtype=jnp.int32)
    positions = jnp.where(local < TXT_DEV, 0, offsets[0] + local - TXT_DEV).astype(jnp.float32)
    half = head // 2
    freqs = jnp.power(10000.0, -jnp.arange(half, dtype=jnp.float32) / half)
    angle = positions[:, None] * freqs[None, :]
    cosine = jnp.concatenate([jnp.cos(angle), jnp.cos(angle)], axis=-1)[:, None, :]
    sine = jnp.concatenate([jnp.sin(angle), jnp.sin(angle)], axis=-1)[:, None, :]
    query = rotate(query, cosine, sine).astype(jnp.bfloat16)
    key_new = rotate(key_new, cosine, sine)
    fresh = jnp.stack([key_new, value_new]).reshape(2, rows, heads * head)
    mine = lax.dynamic_slice_in_dim(stale, lax.axis_index("patch") * rows, rows, 1).astype(
        jnp.float32
    )
    limit = 127.0 * jnp.exp2(exponents[:, 0, :].astype(jnp.float32))
    limit = jnp.repeat(limit, head, axis=1)[:, None, :]
    change = jnp.clip(fresh - mine, -limit, limit).astype(jnp.bfloat16)
    changes = lax.all_gather(change, "patch", axis=1, tiled=True)
    total = stale.shape[1]
    keys = (stale[0].astype(jnp.float32) + changes[0].astype(jnp.float32)).astype(jnp.bfloat16)
    values = (stale[1].astype(jnp.float32) + changes[1].astype(jnp.float32)).astype(jnp.bfloat16)
    keys = keys.reshape(total, heads, head)
    values = values.reshape(total, heads, head)
    index = jnp.arange(total, dtype=jnp.int32)
    within = index % rows
    usable = (within >= TXT_DEV) | (index // rows * TXT_DEV + within < text_count[0])
    scale = head ** (-0.5)
    pieces = []
    for slot in range(heads):
        scores = (
            lax.dot_general(
                query[:, slot],
                keys[:, slot],
                (((1,), (1,)), ((), ())),
                preferred_element_type=jnp.float32,
            )
            * scale
        )
        scores = jnp.where(usable[None, :], scores, -1e30)
        peak = jnp.max(scores, axis=-1, keepdims=True)
        weights = jnp.exp(scores - peak)
        weights = (weights / jnp.sum(weights, axis=-1, keepdims=True)).astype(jnp.bfloat16)
        pieces.append(jnp.dot(weights, values[:, slot], preferred_element_type=jnp.float32))
    attended = jnp.concatenate(pieces, axis=-1).astype(jnp.bfloat16)
    projected = lax.dot_general(
        attended,
        lax.all_gather(w_out, "patch", axis=0, tiled=True),
        (((1,), (1,)), ((), ())),
        preferred_element_type=jnp.float32,
    )
    summed = lax.psum(projected.astype(jnp.bfloat16), "tensor").astype(jnp.float32)
    share = lax.dynamic_slice_in_dim(summed, lax.axis_index("tensor") * own_width, own_width, 1)
    gate = modulation[2].astype(jnp.float32)
    return (hidden.astype(jnp.float32) + gate * share).astype(jnp.bfloat16)


def kernel(
    hidden, mods, w_qkv, w_out, gain, stale, freqs, offsets, text_count, exponents, out,
    hbuf, modbuf, wbuf, wobuf, metasrc, meta, stbuf, normed, mixed, cosbuf, sinbuf, kv, att, abuf, res, landed,
    h_send, h_recv, hf_send, m_send, m_recv, w_send, w_recv, wl_send, wf_send, wo_send, wo_recv,
    me_send, me_recv, st_send, st_recv, kv_send, kv_recv, a_send, a_recv, r_send, r_recv,
):
    g = lax.axis_index("groups")
    z = lax.axis_index("patch")
    t = lax.axis_index("tensor")
    x = t // 2
    c = t % 2
    lead = z // 2
    rows, width = hidden.shape
    quarter = width // 4
    chunk = rows // CHUNKS
    band = rows // BANDS
    head = stale.shape[2] // 2
    mine = 2 * rows
    leading = c == lead

    def remote(src, dst, send, recv, device):
        return pltpu.make_async_remote_copy(
            src_ref=src, dst_ref=dst, send_sem=send, recv_sem=recv, device_id=device, device_id_type=MESH
        )

    sibling = (g, z, 2 * x + 1 - c)

    def arrived(ref, sem):
        remote(ref, ref, st_send.at[0], sem, sibling).wait_recv()

    def left(ref, sem):
        remote(ref, ref, sem, st_recv.at[0], sibling).wait_send()

    modbuf[t, 0:3, :] = mods[...].astype(F32)
    for hl in range(2):
        for kind in range(2):
            scale = jnp.exp2(jnp.full((1, head), exponents[kind, 0, hl], jnp.int32).astype(F32))
            scale = jnp.floor(scale * 65536.0 + 0.5) * (1.0 / 65536.0)
            metasrc[hl, kind : kind + 1, :] = 127.0 * scale
            metasrc[hl, 2 + kind : 3 + kind, :] = gain[kind, hl : hl + 1, :]
        metasrc[hl, 4:5, :] = jnp.full((1, head), offsets[0], jnp.int32).astype(F32)

    barrier = pltpu.get_barrier_semaphore()
    for dz in range(4):
        for dt in range(4):
            if dz or dt:
                pl.semaphore_signal(
                    barrier, inc=1, device_id=(g, (z + dz) % 4, (t + dt) % 4), device_id_type=MESH
                )
    pl.semaphore_signal(barrier, inc=1, device_id=(1 - g, z, t), device_id_type=MESH)
    pl.semaphore_wait(barrier, 16)

    target = z // 2
    j_mine = z % 2

    def part_of(j, ts, k):
        return hbuf.at[j, ts, pl.ds(k * chunk, chunk)]

    for hl in range(2):
        zt = 2 * c + hl

        @pl.when(zt != z)
        def _():
            for core in range(2):
                remote(
                    w_qkv.at[pl.ds((2 * g + core) * quarter, quarter), pl.ds(hl * 3 * head, 3 * head)],
                    wbuf.at[z, 2 * g + core],
                    w_send.at[hl, core],
                    w_recv.at[z, 2 * g + core],
                    (g, zt, 2 * x + core),
                ).start()
            remote(metasrc.at[hl], meta.at[j_mine], me_send.at[hl], me_recv.at[j_mine],
                   (g, zt, 2 * x + target)).start()

    for k in range(CHUNKS):
        piece = hidden.at[pl.ds(k * chunk, chunk)]
        place = part_of(j_mine, t, k)
        got = h_recv.at[j_mine, t, k]

        @pl.when(z < 3)
        def _():
            remote(piece, place, h_send.at[0, k], got, (g, z + 1, 2 * x + target)).start()

        @pl.when(z > 0)
        def _():
            remote(piece, place, h_send.at[1, k], got, (g, z - 1, 2 * x + target)).start()

        remote(piece, place, h_send.at[2, k], got, (g, z, 2 * (1 - x) + target)).start()

        @pl.when(c != target)
        def _():
            remote(piece, place, h_send.at[3, k], got, sibling).start()

    for d in range(1, 4):
        remote(modbuf.at[t], modbuf.at[t], m_send.at[d], m_recv.at[t], (g, z, (t + d) % 4)).start()

    for hl in range(2):
        @pl.when(jnp.logical_and(leading, z % 2 == hl))
        def _():
            for part in range(4):
                remote(
                    w_qkv.at[pl.ds(part * quarter, quarter), pl.ds(hl * 3 * head, 3 * head)],
                    wbuf.at[z, part],
                    wl_send.at[part],
                    w_recv.at[z, part],
                    sibling,
                ).start()
                wbuf[z, part] = w_qkv[pl.ds(part * quarter, quarter), pl.ds(hl * 3 * head, 3 * head)]
            remote(
                stale.at[:, pl.ds(pl.multiple_of((1 - c) * mine, 16), mine), pl.ds(hl * head, head)],
                stbuf, st_send.at[0], st_recv.at[0], sibling,
            ).start()
            stbuf[...] = stale[:, pl.ds(pl.multiple_of(c * mine, 16), mine), pl.ds(hl * head, head)]
            meta[hl] = metasrc[hl]

    @pl.when(c == target)
    def _():
        hbuf[j_mine, t] = hidden[...]

    half_out = width // 2
    across = 2 * (1 - x) + c

    def send_out():
        remote(
            w_out.at[pl.ds(g * half_out, half_out)], wobuf.at[t, g], wo_send.at[0], wo_recv.at[t, g],
            (g, z, across),
        ).start()
        for part in range(2):
            remote(
                w_out.at[pl.ds(part * half_out, half_out)], wobuf.at[t, part], wo_send.at[1 + part],
                wo_recv.at[t, part], sibling,
            ).start()
            wobuf[t, part] = w_out[pl.ds(part * half_out, half_out)]

    def pass_out():
        slot, got = wobuf.at[across, g], wo_recv.at[across, g]
        arrived(slot, got)
        remote(slot, slot, wo_send.at[3], got, (1 - g, z, t)).start()
        remote(slot, slot, wo_send.at[4], got, sibling).start()

    def pass_out_far():
        slot, got = wobuf.at[across, 1 - g], wo_recv.at[across, 1 - g]
        arrived(slot, got)
        remote(slot, slot, wo_send.at[5], got, sibling).start()

    first_j = jnp.where(c == 0, jnp.where(z == 0, 0, 1), jnp.where(z == 3, 1, 0))

    def pass_hidden(order):
        j = first_j if order == 0 else 1 - first_j
        p = 2 * c + j
        onward = jnp.where(z > p, z + 1, z - 1)

        @pl.when(p != z)
        def _():
            for k in range(CHUNKS):
                for cs in range(2):
                    slot, got = part_of(j, 2 * x + cs, k), h_recv.at[j, 2 * x + cs, k]
                    arrived(slot, got)

                    @pl.when(jnp.logical_and(onward >= 0, onward < 4))
                    def _():
                        remote(slot, slot, hf_send.at[order, cs, k, 0], got, (g, (onward + 4) % 4, t)).start()

                    remote(slot, slot, hf_send.at[order, cs, k, 1], got, (g, z, across)).start()

    def pass_weight(d):
        zs = (z + d) % 4
        slot, got = wbuf.at[zs, 2 * g + c], w_recv.at[zs, 2 * g + c]
        arrived(slot, got)
        remote(slot, slot, wf_send.at[d, 0], got, (1 - g, z, t)).start()
        remote(slot, slot, wf_send.at[d, 1], got, sibling).start()

    def pass_weight_far(d):
        zs = (z + d) % 4
        slot, got = wbuf.at[zs, 2 * (1 - g) + c], w_recv.at[zs, 2 * (1 - g) + c]
        arrived(slot, got)
        remote(slot, slot, wf_send.at[d, 2], got, sibling).start()

    def rotary():
        place = lax.broadcasted_iota(jnp.int32, (rows, head), 0)
        lane = lax.broadcasted_iota(jnp.int32, (rows, head), 1)
        for j in range(2):
            @pl.when(jnp.logical_not(jnp.logical_and(leading, z % 2 == j)))
            def _():
                arrived(meta.at[j], me_recv.at[j])

            positions = jnp.where(place < TXT_DEV, 0.0, meta[j, 4:5, :] + (place - TXT_DEV).astype(F32))
            angle = positions * freqs[...]
            cosbuf[pl.ds(j * rows, rows), :] = jnp.cos(angle)
            sine = jnp.sin(angle)
            sinbuf[pl.ds(j * rows, rows), :] = jnp.where(lane < head // 2, -sine, sine)

    def shifts():
        for d in range(1, 4):
            arrived(modbuf.at[(t + d) % 4], m_recv.at[(t + d) % 4])

    features = 4 * width

    def normalise(j):
        for k in range(CHUNKS):
            for cs in range(2):
                arrived(part_of(j, 2 * (1 - x) + cs, k), h_recv.at[j, 2 * (1 - x) + cs, k])

            @pl.when(z == 2 * c + j)
            def _():
                arrived(part_of(j, 2 * x + 1 - c, k), h_recv.at[j, 2 * x + 1 - c, k])

        @pl.loop(0, rows // 16)
        def _(i):
            at = pl.ds(pl.multiple_of(i * 16, 16), 16)
            xs = [hbuf[j, k, at, :].astype(F32) for k in range(4)]
            total = sum(jnp.sum(v, axis=-1, keepdims=True) for v in xs)
            mean = total * (1.0 / features)
            xs = [v - mean for v in xs]
            total = sum(jnp.sum(v * v, axis=-1, keepdims=True) for v in xs)
            inverse = lax.rsqrt(total * (1.0 / features) + 1e-06)
            to = pl.ds(pl.multiple_of(j * rows + i * 16, 16), 16)
            for k in range(4):
                value = xs[k] * inverse * (1.0 + modbuf[k, 1:2, :]) + modbuf[k, 0:1, :]
                normed[to, pl.ds(k * width, width)] = value.astype(BF16)

    pass_hidden(0)
    pass_weight(1)
    pass_weight(3)
    pass_hidden(1)
    pass_weight(2)
    rotary()
    pass_weight_far(1)
    pass_weight_far(3)
    shifts()
    normalise(first_j)
    pass_weight_far(2)
    send_out()
    normalise(1 - first_j)

    for zs in range(4):
        for core in range(2):
            quarter_at = 2 * core + 1 - c

            @pl.when(jnp.logical_not(jnp.logical_and(leading, zs == z)))
            def _():
                arrived(wbuf.at[zs, quarter_at], w_recv.at[zs, quarter_at])

            @pl.when(jnp.logical_and(jnp.logical_not(leading), zs == z))
            def _():
                arrived(wbuf.at[zs, 2 * core + c], w_recv.at[zs, 2 * core + c])

        value = jnp.dot(
            normed[:, pl.ds(zs * width, width)], wbuf[zs].reshape(width, 3 * head), preferred_element_type=F32
        )
        if zs:
            mixed[...] += value
        else:
            mixed[...] = value
    pass_out()

    @pl.when(jnp.logical_not(leading))
    def _():
        arrived(stbuf, st_recv.at[0])

    def rms(values, row):
        root = lax.rsqrt(jnp.mean(values * values, axis=-1, keepdims=True) + 1e-06)
        return values * root * meta[0, row : row + 1, :]

    def turn(values):
        return values * cosbuf[...] + pltpu.roll(values, head // 2, 1) * sinbuf[...]

    second = lax.broadcasted_iota(jnp.int32, (mine, head), 0) >= rows
    ours = pl.ds(pl.multiple_of(c * mine, 16), mine)
    key_new = turn(rms(mixed[:, head : 2 * head], 3))
    for kind, fresh in enumerate((key_new, mixed[:, 2 * head : 3 * head])):
        limit = jnp.where(second, meta[1, kind : kind + 1, :], meta[0, kind : kind + 1, :])
        old = stbuf[kind].astype(F32)
        change = jnp.clip(fresh - old, -limit, limit).astype(BF16)
        kv[kind, ours, :] = (old + change.astype(F32)).astype(BF16)
    remote(kv.at[:, ours, :], kv.at[:, ours, :], kv_send.at[0], kv_recv.at[0], sibling).start()
    query = turn(rms(mixed[:, 0:head], 2)).astype(BF16)
    pass_out_far()
    theirs = pl.ds(pl.multiple_of((1 - c) * mine, 16), mine)
    arrived(kv.at[:, theirs, :], kv_recv.at[0])

    keys = kv[0]
    values = kv[1]
    index = lax.broadcasted_iota(jnp.int32, (1, 2 * mine), 1)
    within = index % rows
    usable = (within >= TXT_DEV) | (index // rows * TXT_DEV + within < text_count[0])
    my_head = 4 * x + z
    for j in range(2):
        scores = lax.dot_general(
            query[j * rows : (j + 1) * rows], keys, (((1,), (1,)), ((), ())), preferred_element_type=F32
        ) * (head ** (-0.5))
        scores = jnp.where(usable, scores, -1e30)
        peak = jnp.max(scores, axis=-1, keepdims=True)
        weights = jnp.exp(scores - peak)
        weights = (weights / jnp.sum(weights, axis=-1, keepdims=True)).astype(BF16)
        att[j] = jnp.dot(weights, values, preferred_element_type=F32).astype(BF16)

    for n in range(BANDS):
        at = pl.ds(n * band, band)
        for j in range(2):
            source, place, got = att.at[j, at], abuf.at[my_head, at], a_recv.at[my_head, n]
            for d in range(1, 4):
                remote(source, place, a_send.at[j, d, n], got, (g, (z + d) % 4, 2 * j + c)).start()

            @pl.when(x != j)
            def _():
                remote(source, place, a_send.at[j, 0, n], got, (g, z, 2 * j + c)).start()

    @pl.when(x == 0)
    def _():
        abuf[my_head] = att[0]

    @pl.when(x == 1)
    def _():
        abuf[my_head] = att[1]

    for part in range(2):
        for ts in (2 * x + 1 - c, 2 * (1 - x) + 1 - c):
            arrived(wobuf.at[ts, part], wo_recv.at[ts, part])
    owner = 2 * c + x
    home = jnp.logical_and(owner == z, z == t)
    for n in range(BANDS):
        at = pl.ds(n * band, band)
        for h in range(8):
            @pl.when(h != my_head)
            def _():
                arrived(abuf.at[h, at], a_recv.at[h, n])

        total = None
        for k in range(4):
            pair = jnp.concatenate([abuf[2 * k, at], abuf[2 * k + 1, at]], axis=-1)
            value = lax.dot_general(
                pair, wobuf[k].reshape(width, 2 * head), (((1,), (1,)), ((), ())), preferred_element_type=F32
            )
            total = value if total is None else total + value
        res[at] = (hbuf[x, z, at].astype(F32) + modbuf[z, 2:3, :] * total).astype(BF16)

        @pl.when(home)
        def _():
            landed[at] = res[at]

        @pl.when(jnp.logical_not(home))
        def _():
            remote(res.at[at], landed.at[at], r_send.at[n], r_recv.at[n], (g, owner, z)).start()

    from_self = jnp.logical_and(t == z, 2 * (z % 2) + z // 2 == t)
    for n in range(BANDS):
        @pl.when(jnp.logical_not(from_self))
        def _():
            arrived(landed.at[pl.ds(n * band, band)], r_recv.at[n])

    out[...] = landed[...]

    for hl in range(2):
        @pl.when(2 * c + hl != z)
        def _():
            for core in range(2):
                left(wbuf.at[z, 2 * g + core], w_send.at[hl, core])
            left(metasrc.at[hl], me_send.at[hl])
    for d in range(1, 4):
        left(modbuf.at[t], m_send.at[d])
        for k in range(2):
            left(wbuf.at[(z + d) % 4, 2 * g + c], wf_send.at[d, k])
        left(wbuf.at[(z + d) % 4, 2 * (1 - g) + c], wf_send.at[d, 2])
        for j in range(2):
            for n in range(BANDS):
                left(att.at[j, pl.ds(n * band, band)], a_send.at[j, d, n])
    for k in range(6):
        left(wobuf.at[t, 0], wo_send.at[k])
    for k in range(CHUNKS):
        piece = hidden.at[pl.ds(k * chunk, chunk)]

        @pl.when(z < 3)
        def _():
            left(piece, h_send.at[0, k])

        @pl.when(z > 0)
        def _():
            left(piece, h_send.at[1, k])

        left(piece, h_send.at[2, k])

        @pl.when(c != target)
        def _():
            left(piece, h_send.at[3, k])

    @pl.when(leading)
    def _():
        for part in range(4):
            left(wbuf.at[z, part], wl_send.at[part])
        left(stbuf, st_send.at[0])

    for order in range(2):
        j = first_j if order == 0 else 1 - first_j
        p = 2 * c + j
        onward = jnp.where(z > p, z + 1, z - 1)

        @pl.when(p != z)
        def _():
            for k in range(CHUNKS):
                for cs in range(2):
                    slot = part_of(j, 2 * x + cs, k)

                    @pl.when(jnp.logical_and(onward >= 0, onward < 4))
                    def _():
                        left(slot, hf_send.at[order, cs, k, 0])

                    left(slot, hf_send.at[order, cs, k, 1])

    for j in range(2):
        @pl.when(x != j)
        def _():
            for n in range(BANDS):
                left(att.at[j, pl.ds(n * band, band)], a_send.at[j, 0, n])
    left(kv.at[:, ours, :], kv_send.at[0])

    @pl.when(jnp.logical_not(home))
    def _():
        for n in range(BANDS):
            left(res.at[pl.ds(n * band, band)], r_send.at[n])


def body(hidden, modulation, w_qkv, w_out, qk_gain, stale, offsets, text_count, exponents):
    rows, width = hidden.shape
    head = w_qkv.shape[2] // 3
    half = head // 2
    freqs = np.power(10000.0, -np.arange(half) / half).astype(np.float32)
    freqs = jnp.asarray(np.concatenate([freqs, freqs])[None])
    dma = pltpu.SemaphoreType.DMA
    vmem = pl.BlockSpec(memory_space=pltpu.VMEM)
    smem = pl.BlockSpec(memory_space=pltpu.SMEM)
    return pl.pallas_call(
        kernel,
        out_shape=jax.ShapeDtypeStruct((rows, width), BF16),
        in_specs=[vmem] * 7 + [smem] * 3,
        out_specs=vmem,
        scratch_shapes=[
            pltpu.VMEM((2, 4, rows, width), BF16),
            pltpu.VMEM((4, 8, width), F32),
            pltpu.VMEM((4, 4, width // 4, 3 * head), BF16),
            pltpu.VMEM((4, 2, width // 2, 2 * head), BF16),
            pltpu.VMEM((2, 8, head), F32),
            pltpu.VMEM((2, 8, head), F32),
            pltpu.VMEM((2, 2 * rows, head), BF16),
            pltpu.VMEM((2 * rows, 4 * width), BF16),
            pltpu.VMEM((2 * rows, 3 * head), F32),
            pltpu.VMEM((2 * rows, head), F32),
            pltpu.VMEM((2 * rows, head), F32),
            pltpu.VMEM((2, 4 * rows, head), BF16),
            pltpu.VMEM((2, rows, head), BF16),
            pltpu.VMEM((8, rows, head), BF16),
            pltpu.VMEM((rows, width), BF16),
            pltpu.VMEM((rows, width), BF16),
            dma((4, CHUNKS)), dma((2, 4, CHUNKS)), dma((2, 2, CHUNKS, 2)), dma((4,)), dma((4,)),
            dma((2, 2)), dma((4, 4)), dma((4,)), dma((4, 3)), dma((6,)), dma((4, 2)),
            dma((2,)), dma((2,)), dma((1,)), dma((1,)), dma((1,)), dma((1,)),
            dma((2, 4, BANDS)), dma((8, BANDS)), dma((BANDS,)), dma((BANDS,)),
        ],
        compiler_params=pltpu.CompilerParams(
            collective_id=0, has_side_effects=True, vmem_limit_bytes=40 * 2**20
        ),
    )(
        hidden, modulation, w_qkv.reshape(w_qkv.shape[0], -1), w_out, qk_gain, stale, freqs,
        offsets, text_count, exponents,
    )


def solution(mesh):
    in_specs = (
        P(("groups", "patch"), "tensor"),
        P(None, "tensor"),
        P("patch", "tensor", None),
        P("patch", "tensor"),
        P(None, "tensor", None),
        P(None, "groups", "tensor"),
        P(("groups", "patch")),
        P("groups"),
        P(None, ("groups", "patch"), "tensor"),
    )
    out_specs = P(("groups", "patch"), "tensor")
    small = (mesh.shape["groups"], mesh.shape["patch"], mesh.shape["tensor"]) == (2, 4, 4)
    return jax.shard_map(
        body if small else plain_body, mesh=mesh, in_specs=in_specs, out_specs=out_specs, check_vma=False
    )
```
